32 devices in a mesh: seq: 4 (over y, x), fsdp: 8 (over z, core).
Axes of the slice: x: 2, y: 2, z: 4, core: 2. Of those that a mesh axis runs over, the one named last changes fastest.
Arguments:
- tokens: bfloat16 [8, 1024, 2048], P('fsdp', 'seq'), may hold values from -6 to 6
- cotangent: bfloat16 [8, 1024, 2048], P('fsdp', 'seq'), may hold values from -6 to 6
- attn_gain: bfloat16 [2048], P('fsdp'), may hold values from 0.5 to 1.5
- attn_shift: bfloat16 [2048], P('fsdp'), may hold values from -1.25 to 1.25
- mlp_gain: bfloat16 [2048], P('fsdp'), may hold values from 0.5 to 1.5
- mlp_shift: bfloat16 [2048], P('fsdp'), may hold values from -1.25 to 1.25
- qkv_weight: bfloat16 [2048, 6144], P('fsdp'), may hold values from -0.375 to 0.375
- qkv_bias: bfloat16 [6144], P('fsdp'), may hold values from -1.25 to 1.25
- dense_weight: bfloat16 [2048, 2048], P('fsdp'), may hold values from -0.5 to 0.5
- dense_bias: bfloat16 [2048], P('fsdp'), may hold values from -1.25 to 1.25
- expand_weight: bfloat16 [2048, 8192], P(None, 'fsdp'), may hold values from -0.125 to 0.125
- expand_bias: bfloat16 [8192], P('fsdp'), may hold values from -1.25 to 1.25
- contract_weight: bfloat16 [8192, 2048], P('fsdp'), may hold values from -0.0625 to 0.0625
- contract_bias: bfloat16 [2048], P('fsdp'), may hold values from -1.25 to 1.25
Outputs:
- block_out: bfloat16 [8, 1024, 2048], P('fsdp', 'seq')
- input_grad: float32 [8, 1024, 2048], P('fsdp', 'seq')
- attngain_grad: float32 [2048], P('fsdp')
- attnshift_grad: float32 [2048], P('fsdp')
- mlpgain_grad: float32 [2048], P('fsdp')
- mlpshift_grad: float32 [2048], P('fsdp')
- qkvweight_grad: float32 [2048, 6144], P('fsdp')
- qkvbias_grad: float32 [6144], P('fsdp')
- denseweight_grad: float32 [2048, 2048], P('fsdp')
- densebias_grad: float32 [2048], P('fsdp')
- expandweight_grad: float32 [2048, 8192], P(None, 'fsdp')
- expandbias_grad: float32 [8192], P('fsdp')
- contractweight_grad: float32 [8192, 2048], P('fsdp')
- contractbias_grad: float32 [2048], P('fsdp')
The draws below stay inside these ranges and needn't reach their ends.
All inputs are finite; a program needn't handle non-finite values.
Results may differ from the reference program's by a relative error of at most 0.0075.
The reference program's roundings to bfloat16 on the way count: a program that leaves them out, or rounds other values in their place, can miss the bound.
Values may be sent and summed in bfloat16 or wider, within the bound.
A program may use at most 384 MiB of HBM per device.

```python
import math
import jax
import jax.numpy as jnp
from jax import lax

D = 2048
FF = 8192
HEADS = 8
HEAD_DIM = 256
ROT = 64
SEQ_LEN = 1024
SEQS = 8


def raised(array, key, source, target, parts, factor):
    def block_of(axis_at):
        return (jnp.arange(array.shape[axis_at]) // (array.shape[axis_at] // parts)).reshape((-1,) + (1,) * (array.ndim - 1 - axis_at))

    near = jax.random.permutation(key, parts)[block_of(target)]
    far = (block_of(target) + parts // 2) % parts
    return jnp.where((block_of(source) == near) | (block_of(source) == far), factor * array, array)


def shard_levels(rng, dims, split, low, high):
    def one(position, blocks):
        steps = jax.random.uniform(jax.random.fold_in(jax.random.fold_in(rng, 6), position), (blocks,), jnp.float32, low / len(split), high / len(split))
        return jnp.repeat(jnp.exp(steps), dims[position] // blocks).reshape((-1,) + (1,) * (len(dims) - position - 1))

    gain = one(*split[0])
    for cut in split[1:]:
        gain = gain * one(*cut)
    return gain


def centred(rng, dims, scale, most, pieces=(), kind=jnp.bfloat16):
    entries = jax.random.normal(rng, dims, jnp.float32) * scale
    if len(pieces) > 0:
        entries = shard_levels(rng, dims, pieces, -0.22, 0.18) * entries
    return jnp.clip(entries, min=-most, max=most).astype(kind)


def bell_draw_with(own_key, extent, scale, most, cuts, heavy, held_as=jnp.bfloat16):
    drawn = scale * jax.random.normal(own_key, extent, jnp.float32)
    if cuts:
        drawn = drawn * shard_levels(own_key, extent, cuts, -0.22, 0.18)
    return jnp.clip(raised(drawn, jax.random.fold_in(own_key, 3), *heavy), -most, most).astype(held_as)


def setup_inputs(seed: int = 0) -> dict:
    key_list = jax.random.split(jax.random.key(seed), 15)
    return {
        "tokens": centred(key_list[0], (SEQS, SEQ_LEN, D), 1.0, 6.0, ((0, 8), (1, 4))),
        "cotangent": bell_draw_with(key_list[1], (SEQS, SEQ_LEN, D), 1.0, 6.0, ((0, 8), (1, 4)), (0, 2, 8, 2.0)),
        "attn_gain": jnp.clip(1.0 + 0.1 * jax.random.normal(key_list[2], (D,), jnp.float32), 0.5, 1.5).astype(jnp.bfloat16),
        "attn_shift": centred(key_list[3], (D,), 0.2, 1.25, ((0, 8),)),
        "mlp_gain": jnp.clip(1.0 + 0.1 * jax.random.normal(key_list[4], (D,), jnp.float32), 0.5, 1.5).astype(jnp.bfloat16),
        "mlp_shift": centred(key_list[5], (D,), 0.2, 1.25, ((0, 8),)),
        "qkv_weight": centred(key_list[6], (D, 3 * D), (D // 8) ** -0.5, 0.375, ((0, 8),)),
        "qkv_bias": centred(key_list[7], (3 * D,), 0.2, 1.25, ((0, 8),)),
        "dense_weight": centred(key_list[8], (D, D), (max(D // 16, 4)) ** -0.5, 0.5, ((0, 8),)),
        "dense_bias": centred(key_list[9], (D,), 0.2, 1.25, ((0, 8),)),
        "expand_weight": centred(key_list[10], (D, FF), D ** -0.5, 0.125, ((1, 8),)),
        "expand_bias": centred(key_list[11], (FF,), 0.2, 1.25, ((0, 8),)),
        "contract_weight": centred(key_list[12], (FF, D), FF ** -0.5, 0.0625, ((0, 8),)),
        "contract_bias": centred(key_list[13], (D,), 0.2, 1.25, ((0, 8),)),
    }


EPSILON = 1e-05

@jax.custom_vjp
def low(v):
    return lax.optimization_barrier(v.astype(jnp.bfloat16)).astype(jnp.float32)

@jax.custom_vjp
def low_back(v):
    return v

def low_keep(v):
    return (low(v), None)

def low_pass(kept, grad):
    return (grad,)

def back_keep(v):
    return (v, None)

def back_low(kept, grad):
    return (low(grad),)
low.defvjp(low_keep, low_pass)
low_back.defvjp(back_keep, back_low)

def layer_norm(values, ln_gain, ln_shift):
    center = lax.optimization_barrier(jnp.mean(values, axis=-1, keepdims=True))
    offset_rows = values - center
    spread = lax.optimization_barrier(jnp.mean(offset_rows * offset_rows, axis=-1, keepdims=True))
    return offset_rows * lax.rsqrt(spread + EPSILON) * ln_gain + ln_shift

def rotary_tables(positions):
    frequency = 1.0 / 10000.0 ** (jnp.arange(0, ROT, 2, dtype=jnp.float32) / ROT)
    angles = positions.astype(jnp.float32)[:, None] * frequency[None, :]
    return (jnp.cos(angles)[:, None, :], jnp.sin(angles)[:, None, :])

def rotate(head_rows, cosine, sine):
    half_rot = ROT // 2
    first_half = head_rows[..., :half_rot]
    second = head_rows[..., half_rot:ROT]
    return jnp.concatenate([first_half * cosine - second * sine, second * cosine + first_half * sine, head_rows[..., ROT:]], axis=-1)

def matmul(left, right):
    return jnp.dot(left, right, precision=lax.Precision.HIGHEST, preferred_element_type=jnp.float32)

def forward(x_rows, attn_gain, attn_shift, mlp_gain, mlp_shift, qkv_weight, qkv_bias, dense_weight, dense_bias, expand_weight, expand_bias, contract_weight, contract_bias):
    group_size, length, feat_width = x_rows.shape
    attn_in = low(layer_norm(x_rows, attn_gain, attn_shift))
    projected = low_back(matmul(attn_in, qkv_weight) + qkv_bias).reshape(group_size, length, 3, HEADS, HEAD_DIM)
    cosine_table, sine_table = rotary_tables(lax.iota(jnp.int32, length))
    queries = low(low_back(rotate(projected[:, :, 0], cosine_table, sine_table)))
    key_rows = low(low_back(rotate(projected[:, :, 1], cosine_table, sine_table)))
    value_rows = low(low_back(projected[:, :, 2]))
    scores = jnp.einsum('gqhd,gkhd->ghqk', queries, key_rows, precision=lax.Precision.HIGHEST) * HEAD_DIM ** (-0.5)
    scores = low_back(scores)
    causal = lax.iota(jnp.int32, length)[:, None] >= lax.iota(jnp.int32, length)[None, :]
    scores = jnp.where(causal, scores, -jnp.inf)
    attn_probs = low(jax.nn.softmax(scores, axis=-1))
    context = jnp.einsum('ghqk,gkhd->gqhd', attn_probs, value_rows, precision=lax.Precision.HIGHEST)
    context = low(low_back(context.reshape(group_size, length, feat_width)))
    attn_out = matmul(context, dense_weight) + dense_bias
    mlp_in = low(layer_norm(x_rows, mlp_gain, mlp_shift))
    pre_act = low_back(matmul(mlp_in, expand_weight) + expand_bias)
    act_low = low(jax.nn.gelu(pre_act, approximate=False))
    mlp_out = matmul(act_low, contract_weight) + contract_bias
    return x_rows + attn_out + mlp_out

def reference(tokens, cotangent, attn_gain, attn_shift, mlp_gain, mlp_shift, qkv_weight, qkv_bias, dense_weight, dense_bias, expand_weight, expand_bias, contract_weight, contract_bias):
    group_size = math.gcd(SEQS, max(1, 4096 // SEQ_LEN))
    group_count = SEQS // group_size
    weights = tuple((weight_arg.astype(jnp.float32) for weight_arg in (attn_gain, attn_shift, mlp_gain, mlp_shift, qkv_weight, qkv_bias, dense_weight, dense_bias, expand_weight, expand_bias, contract_weight, contract_bias)))
    token_groups = tokens.astype(jnp.float32).reshape(group_count, group_size, SEQ_LEN, D)
    cotangent_groups = cotangent.astype(jnp.float32).reshape(group_count, group_size, SEQ_LEN, D)

    def one_group(running, group_pair):
        outputs, pullback = jax.vjp(forward, group_pair[0], *weights)
        all_grads = pullback(group_pair[1])
        updated = tuple((summed + addend for summed, addend in zip(running, all_grads[1:])))
        return (updated, (outputs.astype(jnp.bfloat16), all_grads[0]))
    start_grads = tuple((jnp.zeros_like(weight_arg) for weight_arg in weights))
    totals, produced = lax.scan(one_group, start_grads, (token_groups, cotangent_groups))
    block_out = produced[0].reshape(SEQS, SEQ_LEN, D)
    input_grad = produced[1].reshape(SEQS, SEQ_LEN, D)
    return (block_out, input_grad, totals[0], totals[1], totals[2], totals[3], totals[4], totals[5], totals[6], totals[7], totals[8], totals[9], totals[10], totals[11])
```

```python
from functools import partial

import jax
import jax.numpy as jnp
from jax import lax
from jax.experimental import pallas as pl
from jax.experimental.pallas import tpu as pltpu
from jax.sharding import PartitionSpec as P

HEADS = 8
HEAD_DIM = 256
ROT = 64
EPSILON = 1e-05
QUERY_BLOCK = 256


def dot_plain(left, right):
    return jnp.dot(left, right, preferred_element_type=jnp.float32)


def dot_right(left, right):
    return lax.dot_general(
        left, right, (((1,), (1,)), ((), ())), preferred_element_type=jnp.float32
    )


def dot_left(left, right):
    return lax.dot_general(
        left, right, (((0,), (0,)), ((), ())), preferred_element_type=jnp.float32
    )


def rotary_tables(length):
    half = ROT // 2
    frequency = 1.0 / 10000.0 ** (jnp.arange(0, ROT, 2, dtype=jnp.float32) / ROT)
    angles = lax.iota(jnp.int32, length).astype(jnp.float32)[:, None] * frequency[None, :]
    cosine, sine = jnp.cos(angles), jnp.sin(angles)
    zero = jnp.zeros((length, half), jnp.float32)
    rest = 128 - ROT
    return (
        jnp.concatenate([cosine, cosine, jnp.ones((length, rest), jnp.float32)], axis=1),
        jnp.concatenate([-sine, zero, jnp.zeros((length, rest), jnp.float32)], axis=1),
        jnp.concatenate([zero, sine, jnp.zeros((length, rest), jnp.float32)], axis=1),
    )


def rotate(rows, cosine, sine_low, sine_high, sign):
    part = rows[:, :128]
    turned = part * cosine + sign * (
        pltpu.roll(part, 128 - ROT // 2, 1) * sine_low + pltpu.roll(part, ROT // 2, 1) * sine_high
    )
    return jnp.concatenate([turned, rows[:, 128:]], axis=1)


def softmax_block(query_block, key_rows):
    size, width = query_block.shape[0], key_rows.shape[0]
    scores = dot_right(query_block, key_rows) * HEAD_DIM ** (-0.5)
    row = lax.broadcasted_iota(jnp.int32, (size, width), 0) + (width - size)
    column = lax.broadcasted_iota(jnp.int32, (size, width), 1)
    scores = jnp.where(row >= column, scores, -jnp.inf)
    exponent = jnp.exp(scores - jnp.max(scores, axis=-1, keepdims=True))
    return exponent / jnp.sum(exponent, axis=-1, keepdims=True)


VMEM_LIMIT = 56 * 1024 * 1024
ROW_BLOCK = 256
UNIT_BLOCK = 256


def params(**more):
    return pltpu.CompilerParams(vmem_limit_bytes=VMEM_LIMIT, **more)


def light():
    return pl.CostEstimate(flops=1024, bytes_accessed=1024, transcendentals=0)


def normal_rows(values):
    center = jnp.mean(values, axis=-1, keepdims=True)
    offset_rows = values - center
    spread = jnp.mean(offset_rows * offset_rows, axis=-1, keepdims=True)
    inverse = lax.rsqrt(spread + EPSILON)
    return offset_rows * inverse, inverse


def qkv_kernel(
    rotated, x_ref, vec_ref, weight_ref, bias_ref, cos_ref, low_ref, high_ref, attn_ref, mlp_ref, out_ref
):
    normal, _ = normal_rows(x_ref[...].astype(jnp.float32))
    attn_in = (normal * vec_ref[0:1, :] + vec_ref[1:2, :]).astype(jnp.bfloat16)
    attn_ref[...] = attn_in
    mlp_ref[...] = (normal * vec_ref[2:3, :] + vec_ref[3:4, :]).astype(jnp.bfloat16)
    for head in range(weight_ref.shape[1] // HEAD_DIM):
        columns = pl.ds(head * HEAD_DIM, HEAD_DIM)
        value = dot_plain(attn_in, weight_ref[:, columns]) + bias_ref[:, columns]
        if head < rotated:
            value = rotate(value, cos_ref[...], low_ref[...], high_ref[...], 1.0)
        out_ref[:, columns] = value.astype(jnp.bfloat16)


def project_heads(x_rows, vectors, weight, bias, tables, local):
    total, width = x_rows.shape
    heads_width = 3 * local * HEAD_DIM
    cycle = tables[0].shape[0] // ROW_BLOCK
    rows = lambda columns: pl.BlockSpec((ROW_BLOCK, columns), lambda i: (i, 0))
    whole = lambda shape: pl.BlockSpec(shape, lambda i: (0, 0))
    table = pl.BlockSpec((ROW_BLOCK, 128), lambda i: (lax.rem(i, cycle), 0))
    return pl.pallas_call(
        partial(qkv_kernel, 2 * local),
        grid=(total // ROW_BLOCK,),
        out_shape=[
            jax.ShapeDtypeStruct((total, width), jnp.bfloat16),
            jax.ShapeDtypeStruct((total, width), jnp.bfloat16),
            jax.ShapeDtypeStruct((total, heads_width), jnp.bfloat16),
        ],
        in_specs=[
            rows(width),
            whole(vectors.shape),
            whole((width, heads_width)),
            whole((1, heads_width)),
            table,
            table,
            table,
        ],
        out_specs=[rows(width), rows(width), rows(heads_width)],
        compiler_params=params(),
        cost_estimate=light(),
    )(x_rows, vectors, weight, bias, *tables)


def attend_kernel(
    local, qkv_ref, cot_ref, dense_ref, cos_ref, low_ref, high_ref, ctx_ref, out_ref, key_acc, value_acc
):
    length = qkv_ref.shape[0]
    score_scale = HEAD_DIM ** (-0.5)
    for head in range(local):
        columns = pl.ds(head * HEAD_DIM, HEAD_DIM)
        key_columns = pl.ds((local + head) * HEAD_DIM, HEAD_DIM)
        value_columns = pl.ds((2 * local + head) * HEAD_DIM, HEAD_DIM)
        key_acc[...] = jnp.zeros_like(key_acc)
        value_acc[...] = jnp.zeros_like(value_acc)
        for start in range(0, length, QUERY_BLOCK):
            stop = start + QUERY_BLOCK
            query_block = qkv_ref[start:stop, columns]
            grad_block = dot_right(cot_ref[start:stop, :], dense_ref[columns, :]).astype(
                jnp.bfloat16
            )
            probs = softmax_block(query_block, qkv_ref[:stop, key_columns])
            probs_low = probs.astype(jnp.bfloat16)
            ctx_ref[start:stop, columns] = dot_plain(
                probs_low, qkv_ref[:stop, value_columns]
            ).astype(jnp.bfloat16)
            value_acc[:stop, :] += dot_left(probs_low, grad_block)
            probs_grad = dot_right(grad_block, qkv_ref[:stop, value_columns])
            inner_sum = jnp.sum(probs * probs_grad, axis=-1, keepdims=True)
            score_grad = (probs * (probs_grad - inner_sum)).astype(jnp.bfloat16)
            key_acc[:stop, :] += dot_left(score_grad, query_block)
            query_grad = dot_plain(score_grad, qkv_ref[:stop, key_columns]) * score_scale
            query_grad = query_grad.astype(jnp.bfloat16).astype(jnp.float32)
            out_ref[start:stop, columns] = rotate(
                query_grad,
                cos_ref[start:stop, :],
                low_ref[start:stop, :],
                high_ref[start:stop, :],
                -1.0,
            ).astype(jnp.bfloat16)
        key_grad = (key_acc[...] * score_scale).astype(jnp.bfloat16).astype(jnp.float32)
        out_ref[:, key_columns] = rotate(
            key_grad, cos_ref[...], low_ref[...], high_ref[...], -1.0
        ).astype(jnp.bfloat16)
        out_ref[:, value_columns] = value_acc[...].astype(jnp.bfloat16)


def attend(qkv, cot_rows, dense_part, tables, local):
    length = qkv.shape[0]
    vmem = pl.BlockSpec(memory_space=pltpu.VMEM)
    return pl.pallas_call(
        partial(attend_kernel, local),
        out_shape=[
            jax.ShapeDtypeStruct((length, local * HEAD_DIM), jnp.bfloat16),
            jax.ShapeDtypeStruct(qkv.shape, jnp.bfloat16),
        ],
        in_specs=[vmem] * 6,
        out_specs=[vmem] * 2,
        scratch_shapes=[pltpu.VMEM((length, HEAD_DIM), jnp.float32)] * 2,
        compiler_params=params(),
        cost_estimate=light(),
    )(qkv, cot_rows, dense_part, *tables)


def up_kernel(mlp_ref, cot_ref, weight_ref, bias_ref, act_ref, slope_ref, grad_ref):
    pre = dot_right(mlp_ref[...], weight_ref[...]) + bias_ref[...]
    below = 0.5 * (1.0 + lax.erf(pre * 0.5**0.5))
    act = (pre * below).astype(jnp.bfloat16)
    act_ref[...] = act
    slope_ref[...] = below + pre * (0.3989422804014327 * jnp.exp(-0.5 * pre * pre))
    grad_ref[...] = dot_left(act, cot_ref[...]).astype(jnp.bfloat16)


def expand_units(mlp_in, cot_rows, weight, bias):
    total, width = mlp_in.shape
    hidden = weight.shape[0]
    whole = pl.BlockSpec((total, width), lambda j: (0, 0))
    units = pl.BlockSpec((UNIT_BLOCK, width), lambda j: (j, 0))
    column = pl.BlockSpec((total, UNIT_BLOCK), lambda j: (0, j))
    return pl.pallas_call(
        up_kernel,
        grid=(hidden // UNIT_BLOCK,),
        out_shape=[
            jax.ShapeDtypeStruct((total, hidden), jnp.bfloat16),
            jax.ShapeDtypeStruct((total, hidden), jnp.float32),
            jax.ShapeDtypeStruct((hidden, width), jnp.bfloat16),
        ],
        in_specs=[whole, whole, units, pl.BlockSpec((1, UNIT_BLOCK), lambda j: (0, j))],
        out_specs=[column, column, units],
        compiler_params=params(),
        cost_estimate=light(),
    )(mlp_in, cot_rows, weight, bias)


def down_kernel(mlp_ref, cot_ref, weight_ref, slope_ref, pre_ref, grad_ref, sum_ref):
    pre_grad = (dot_right(cot_ref[...], weight_ref[...]) * slope_ref[...]).astype(jnp.bfloat16)
    pre_ref[...] = pre_grad
    grad_ref[...] = dot_left(pre_grad, mlp_ref[...]).astype(jnp.bfloat16)
    sum_ref[...] = jnp.sum(pre_grad.astype(jnp.float32), axis=0, keepdims=True)


def contract_units(mlp_in, cot_rows, weight, slope):
    total, width = mlp_in.shape
    hidden = weight.shape[0]
    whole = pl.BlockSpec((total, width), lambda j: (0, 0))
    units = pl.BlockSpec((UNIT_BLOCK, width), lambda j: (j, 0))
    column = pl.BlockSpec((total, UNIT_BLOCK), lambda j: (0, j))
    return pl.pallas_call(
        down_kernel,
        grid=(hidden // UNIT_BLOCK,),
        out_shape=[
            jax.ShapeDtypeStruct((total, hidden), jnp.bfloat16),
            jax.ShapeDtypeStruct((hidden, width), jnp.bfloat16),
            jax.ShapeDtypeStruct((1, hidden), jnp.float32),
        ],
        in_specs=[whole, whole, units, column],
        out_specs=[column, units, pl.BlockSpec((1, UNIT_BLOCK), lambda j: (0, j))],
        compiler_params=params(),
        cost_estimate=light(),
    )(mlp_in, cot_rows, weight, slope)


def norm_kernel(x_ref, proj_ref, pre_ref, vec_ref, qkv_ref, expand_ref, part_ref, sums_ref):
    normal, _ = normal_rows(x_ref[...].astype(jnp.float32))

    @pl.when(pl.program_id(0) == 0)
    def _():
        sums_ref[...] = jnp.zeros_like(sums_ref)

    grad = dot_right(proj_ref[...], qkv_ref[...])
    sums_ref[0:1, :] += jnp.sum(grad * normal, axis=0, keepdims=True)
    sums_ref[1:2, :] += jnp.sum(grad, axis=0, keepdims=True)
    part = grad * vec_ref[0:1, :]
    grad = dot_plain(pre_ref[...], expand_ref[...])
    sums_ref[2:3, :] += jnp.sum(grad * normal, axis=0, keepdims=True)
    sums_ref[3:4, :] += jnp.sum(grad, axis=0, keepdims=True)
    part_ref[...] = (part + grad * vec_ref[2:3, :]).astype(jnp.bfloat16)


def norm_parts(x_rows, proj_grad, pre_grad, vectors, qkv_part, expand_part):
    total, width = x_rows.shape
    rows = lambda columns: pl.BlockSpec((ROW_BLOCK, columns), lambda i: (i, 0))
    whole = lambda shape: pl.BlockSpec(shape, lambda i: (0, 0))
    return pl.pallas_call(
        norm_kernel,
        grid=(total // ROW_BLOCK,),
        out_shape=[
            jax.ShapeDtypeStruct((total, width), jnp.bfloat16),
            jax.ShapeDtypeStruct((8, width), jnp.float32),
        ],
        in_specs=[
            rows(width),
            rows(proj_grad.shape[1]),
            rows(pre_grad.shape[1]),
            whole(vectors.shape),
            whole((width, proj_grad.shape[1])),
            whole(expand_part.shape),
        ],
        out_specs=[rows(width), whole((8, width))],
        compiler_params=params(),
        cost_estimate=light(),
    )(x_rows, proj_grad, pre_grad, vectors, qkv_part, expand_part)


def out_kernel(ctx_ref, act_ref, dense_ref, contract_ref, out_ref):
    total = dot_plain(act_ref[...], contract_ref[...]) + dot_plain(ctx_ref[...], dense_ref[...])
    out_ref[...] = total.astype(jnp.bfloat16)


def out_parts(context, act, dense_part, contract_part):
    total = context.shape[0]
    width = dense_part.shape[1]
    rows = lambda columns: pl.BlockSpec((ROW_BLOCK, columns), lambda i: (i, 0))
    whole = lambda shape: pl.BlockSpec(shape, lambda i: (0, 0))
    return pl.pallas_call(
        out_kernel,
        grid=(total // ROW_BLOCK,),
        out_shape=jax.ShapeDtypeStruct((total, width), jnp.bfloat16),
        in_specs=[
            rows(context.shape[1]),
            rows(act.shape[1]),
            whole(dense_part.shape),
            whole(contract_part.shape),
        ],
        out_specs=rows(width),
        compiler_params=params(),
        cost_estimate=light(),
    )(context, act, dense_part, contract_part)


def square_kernel(layouts, *refs):
    count = len(layouts)
    blocks, gathered = refs[:count], refs[count : 2 * count]
    own_sem, send_x, recv_x, send_y, recv_y, pass_x, land_x, pass_y, land_y = refs[2 * count :]
    place = lax.axis_index("seq")
    over_x = place + 1 - 2 * lax.rem(place, 2)
    over_y = lax.rem(place + 2, 4)
    barrier = pltpu.get_barrier_semaphore()
    for neighbour in (over_x, over_y):
        pl.semaphore_signal(
            barrier, inc=1, device_id={"seq": neighbour}, device_id_type=pl.DeviceIdType.MESH
        )
    pl.semaphore_wait(barrier, 2)

    pieces = []
    for block, into, layout in zip(blocks, gathered, layouts):
        rows, columns = block.shape
        parts = layout if layout else 1
        each = columns // parts
        for part in range(parts):
            pieces.append((block, into, layout, rows, each, part))

    def view(piece, slot, start, size):
        _, into, layout, rows, each, part = piece
        if not layout:
            first = pl.multiple_of(slot * rows + start, 16)
            return into.at[pl.ds(first, size), :]
        first = pl.multiple_of((part * 4 + slot) * each, 128)
        return into.at[pl.ds(start, size), pl.ds(first, each)]

    def send(source, target, chip, send_sem, recv_sem):
        copy = pltpu.make_async_remote_copy(
            src_ref=source,
            dst_ref=target,
            send_sem=send_sem,
            recv_sem=recv_sem,
            device_id={"seq": chip},
            device_id_type=pl.DeviceIdType.MESH,
        )
        copy.start()
        return copy

    own, to_x, to_y, last = [], [], [], []
    for i, piece in enumerate(pieces):
        block, _, _, rows, each, part = piece
        source = block.at[:, pl.ds(part * each, each)]
        target = view(piece, place, 0, rows)
        to_x.append(send(source, target, over_x, send_x.at[i], recv_x.at[i]))
        to_y.append(send(source, target, over_y, send_y.at[i], recv_y.at[i]))
        copy = pltpu.make_async_copy(source, target, own_sem.at[i])
        copy.start()
        own.append(copy)
    for i, piece in enumerate(pieces):
        half = piece[3] // 2
        to_x[i].wait_recv()
        second = view(piece, over_x, half, half)
        last.append(send(second, second, over_y, pass_y.at[i], land_y.at[i]))
        to_y[i].wait_recv()
        first = view(piece, over_y, 0, half)
        last.append(send(first, first, over_x, pass_x.at[i], land_x.at[i]))
    for copy in last:
        copy.wait()
    for i in range(len(pieces)):
        own[i].wait()
        to_x[i].wait_send()
        to_y[i].wait_send()


def gather_square(blocks, layouts, identity):
    if lax.axis_size("seq") != 4:
        results = []
        for block, layout in zip(blocks, layouts):
            if not layout:
                results.append(lax.all_gather(block, "seq", axis=0, tiled=True))
            else:
                cut = block.reshape(block.shape[0], layout, 1, block.shape[1] // layout)
                full = lax.all_gather(cut, "seq", axis=2, tiled=True)
                results.append(full.reshape(block.shape[0], -1))
        return results
    shapes = [
        jax.ShapeDtypeStruct(
            (4 * b.shape[0], b.shape[1]) if not n else (b.shape[0], 4 * b.shape[1]), b.dtype
        )
        for b, n in zip(blocks, layouts)
    ]
    pieces = sum(max(n, 1) for n in layouts)
    return pl.pallas_call(
        partial(square_kernel, layouts),
        out_shape=shapes,
        in_specs=[pl.BlockSpec(memory_space=pl.ANY)] * len(blocks),
        out_specs=[pl.BlockSpec(memory_space=pl.ANY)] * len(blocks),
        scratch_shapes=[pltpu.SemaphoreType.DMA((pieces,))] * 9,
        compiler_params=pltpu.CompilerParams(collective_id=identity, has_side_effects=True),
        cost_estimate=light(),
    )(*blocks)


def after(array, *others):
    return lax.optimization_barrier((array, *others))[0]


def permute(array, axis, pairs):
    return lax.ppermute(array, axis, pairs)


def line_moves(chips):
    owners = 2 * chips
    up = [(i, i + 2) for i in range(owners - 2)]
    down = [(i + 2, i) for i in range(owners - 2)]
    other = [(i, i ^ 1) for i in range(owners)]
    return up, down, other


def add_low(*terms):
    total = terms[0].astype(jnp.float32)
    for term in terms[1:]:
        total = total + term.astype(jnp.float32)
    return total.astype(terms[0].dtype)


def scatter_owners(parts):
    owners, owner = lax.axis_size("fsdp"), lax.axis_index("fsdp")
    chips, chip, core = owners // 2, owner // 2, lax.rem(owner, 2)
    up, down, other = line_moves(chips)
    by_core = parts.reshape(chips, 2, *parts.shape[1:])
    theirs = lax.dynamic_index_in_dim(by_core, 1 - core, 1, False)
    mine = lax.dynamic_index_in_dim(by_core, core, 1, False)
    sums = add_low(mine, permute(theirs, "fsdp", other))

    def block_for(target):
        return lax.dynamic_index_in_dim(sums, jnp.clip(target, 0, chips - 1), 0, False)

    rising = falling = None
    for step in range(chips - 1, 0, -1):
        send_up, send_down = block_for(chip + step), block_for(chip - step)
        if rising is not None:
            send_up, send_down = add_low(send_up, rising), add_low(send_down, falling)
        rising = permute(send_up, "fsdp", up)
        falling = permute(send_down, "fsdp", down)
    return add_low(block_for(chip), rising, falling)


SQUARE_X = [(i, i ^ 1) for i in range(4)]
SQUARE_Y = [(i, i ^ 2) for i in range(4)]


def scatter_square(parts):
    seqs = lax.axis_size("seq")
    if seqs != 4:
        return lax.psum_scatter(parts, "seq", scatter_dimension=0, tiled=True)
    place, rows = lax.axis_index("seq"), parts.shape[0] // seqs
    half = rows // 2

    def part(target, offset, count):
        return lax.dynamic_slice_in_dim(parts, target * rows + offset, count, 0)

    over_x = permute(part(place ^ 3, 0, half), "seq", SQUARE_X)
    over_y = permute(part(place ^ 3, half, half), "seq", SQUARE_Y)
    to_x = jnp.concatenate(
        [part(place ^ 1, 0, half), add_low(part(place ^ 1, half, half), over_y)], axis=0
    )
    to_y = jnp.concatenate(
        [add_low(part(place ^ 2, 0, half), over_x), part(place ^ 2, half, half)], axis=0
    )
    return add_low(
        part(place, 0, rows), permute(to_x, "seq", SQUARE_X), permute(to_y, "seq", SQUARE_Y)
    )


def sum_square(array):
    if lax.axis_size("seq") != 4:
        return lax.psum(array, "seq")
    array = array + permute(array, "seq", SQUARE_X)
    return array + permute(array, "seq", SQUARE_Y)


def shards(
    tokens,
    cotangent,
    attn_gain,
    attn_shift,
    mlp_gain,
    mlp_shift,
    qkv_weight,
    qkv_bias,
    dense_weight,
    dense_bias,
    expand_weight,
    expand_bias,
    contract_weight,
    contract_bias,
):
    seqs, owners = lax.axis_size("seq"), lax.axis_size("fsdp")
    place, owner = lax.axis_index("seq"), lax.axis_index("fsdp")
    seq_count, local_len, width = tokens.shape
    length = local_len * seqs
    rows_local = seq_count * local_len
    local = HEADS // seqs
    head_width = local * HEAD_DIM
    depth = width // owners
    units = expand_weight.shape[1] // seqs
    hidden = units * owners
    bf16, f32 = jnp.bfloat16, jnp.float32

    def by_sequence(array):
        parts = array.reshape(seqs, seq_count, local_len, width)
        return jnp.swapaxes(parts, 0, 1).reshape(seq_count * length, width)

    def scatter_rows(array):
        parts = array.reshape(seq_count, seqs, local_len, width)
        return scatter_square(jnp.swapaxes(parts, 0, 1).reshape(seqs * rows_local, width))

    attn_own = jnp.concatenate(
        [
            lax.dynamic_slice(
                qkv_weight.reshape(depth, 3, width),
                (0, 0, place * head_width),
                (depth, 3, head_width),
            ).reshape(depth, 3 * head_width),
            lax.dynamic_slice(dense_weight, (0, place * head_width), (depth, head_width)),
        ],
        axis=1,
    )
    expand_own = lax.dynamic_slice(expand_weight, (0, place * units), (width, units)).T
    contract_own = lax.dynamic_slice(contract_weight, (place * units, 0), (units, width))
    attn_part = lax.all_gather(attn_own, "fsdp", axis=0, tiled=True)
    expand_part = lax.all_gather(expand_own, "fsdp", axis=0, tiled=True)
    contract_part = lax.all_gather(contract_own, "fsdp", axis=0, tiled=True)
    dense_part = lax.all_to_all(
        attn_part[:, 3 * head_width :], "seq", split_axis=0, concat_axis=1, tiled=True
    )
    small = jnp.concatenate(
        [
            attn_gain,
            attn_shift,
            mlp_gain,
            mlp_shift,
            dense_bias,
            contract_bias,
            qkv_bias,
            lax.dynamic_slice(expand_bias, (place * units,), (units,)),
        ]
    )
    small = lax.all_gather(small, "fsdp", axis=0, tiled=False).astype(f32)
    vectors = jnp.swapaxes(small[:, : 6 * depth].reshape(owners, 6, depth), 0, 1)
    vectors = jnp.concatenate([vectors.reshape(6, width), jnp.zeros((2, width), f32)], axis=0)
    bias_qkv = small[:, 6 * depth : 9 * depth].reshape(3, seqs, head_width)
    bias_qkv = lax.dynamic_index_in_dim(bias_qkv, place, 1, False).reshape(1, 3 * head_width)
    bias_expand = small[:, 9 * depth :].reshape(1, hidden)

    x_own = tokens.reshape(rows_local, width)
    cot_own = cotangent.reshape(rows_local, width)
    x_rows, cot_rows = [
        by_sequence(rows) for rows in gather_square([x_own, cot_own], (0, 0), 0)
    ]

    tables = rotary_tables(length)
    attn_in, mlp_in, qkv = project_heads(x_rows, vectors, attn_part, bias_qkv, tables, local)
    pairs = [
        attend(
            qkv[item * length : (item + 1) * length],
            cot_rows[item * length : (item + 1) * length],
            dense_part,
            tables,
            local,
        )
        for item in range(seq_count)
    ]
    context = jnp.concatenate([pair[0] for pair in pairs], axis=0)
    proj_grad = jnp.concatenate([pair[1] for pair in pairs], axis=0)
    dense_grad = dot_left(context, cot_rows).astype(bf16)
    dense_grad = lax.all_to_all(dense_grad, "seq", split_axis=1, concat_axis=0, tiled=True)
    qkv_grad = dot_left(attn_in, proj_grad).astype(bf16)
    attn_grad = jnp.concatenate([qkv_grad, dense_grad], axis=1)
    attn_total = lax.psum_scatter(attn_grad, "fsdp", scatter_dimension=0, tiled=True)

    act, slope, contract_grad = expand_units(mlp_in, cot_rows, expand_part, bias_expand)
    contract_total = lax.psum_scatter(contract_grad, "fsdp", scatter_dimension=0, tiled=True)
    pre_grad, expand_grad, expandbias_sum = contract_units(mlp_in, cot_rows, contract_part, slope)
    expand_total = lax.psum_scatter(expand_grad, "fsdp", scatter_dimension=0, tiled=True)

    norm_part, gain_sums = norm_parts(x_rows, proj_grad, pre_grad, vectors, attn_part, expand_part)
    norm_grad = scatter_rows(norm_part).astype(f32)
    normal_own, inverse_own = normal_rows(x_own.astype(f32))
    x_grad = inverse_own * (
        norm_grad
        - jnp.mean(norm_grad, axis=-1, keepdims=True)
        - normal_own * jnp.mean(norm_grad * normal_own, axis=-1, keepdims=True)
    )
    input_grad = cot_own.astype(f32) + x_grad

    out_sum = scatter_rows(out_parts(context, act, dense_part, contract_part)).astype(f32)
    block_out = (x_own.astype(f32) + out_sum + (vectors[4] + vectors[5])).astype(bf16)

    attn_total, contract_total = gather_square([attn_total, contract_total], (4, 0), 1)
    (expand_total,) = gather_square([expand_total.T], (1,), 2)
    qkv_total = attn_total[:, : 3 * width]
    dense_total = attn_total[:, 3 * width :]

    expandbias_sum = lax.dynamic_update_slice(
        jnp.zeros((owners, seqs, units), f32),
        expandbias_sum.reshape(owners, 1, units),
        (0, place, 0),
    )
    qkvbias_sum = jnp.sum(proj_grad.astype(f32), axis=0).reshape(3, 1, head_width)
    qkvbias_sum = lax.dynamic_update_slice(
        jnp.zeros((3, seqs, head_width), f32), qkvbias_sum, (0, place, 0)
    )
    cot_sum = jnp.sum(cot_own.astype(f32), axis=0)
    gain_sums = jnp.swapaxes(gain_sums[:4].reshape(4, owners, depth), 0, 1)
    sums = jnp.concatenate(
        [
            gain_sums.reshape(owners, 4 * depth),
            cot_sum.reshape(owners, depth),
            qkvbias_sum.reshape(owners, 3 * depth),
            expandbias_sum.reshape(owners, seqs * units),
        ],
        axis=1,
    )
    mine = sum_square(scatter_owners(sums.reshape(owners, 1, -1)))[0]
    cuts = [mine[i * depth : (i + 1) * depth] for i in range(5)]
    qkvbias_total = mine[5 * depth : 8 * depth]
    expandbias_total = mine[8 * depth :]
    return (
        block_out.reshape(tokens.shape),
        input_grad.reshape(tokens.shape),
        cuts[0],
        cuts[1],
        cuts[2],
        cuts[3],
        qkv_total.astype(f32),
        qkvbias_total,
        dense_total.astype(f32),
        cuts[4],
        expand_total.astype(f32),
        expandbias_total,
        contract_total.astype(f32),
        cuts[4],
    )


def solution(mesh):
    vector, rows = P("fsdp"), P("fsdp", None)
    tokens = P("fsdp", "seq", None)
    return jax.shard_map(
        shards,
        mesh=mesh,
        in_specs=(
            tokens,
            tokens,
            vector,
            vector,
            vector,
            vector,
            rows,
            vector,
            rows,
            vector,
            P(None, "fsdp"),
            vector,
            rows,
            vector,
        ),
        out_specs=(
            tokens,
            tokens,
            vector,
            vector,
            vector,
            vector,
            rows,
            vector,
            rows,
            vector,
            P(None, "fsdp"),
            vector,
            rows,
            vector,
        ),
        check_vma=False,
    )
```
